32 devices in a mesh: rep: 2 (over x), node: 8 (over z, y), local: 2 (over core).
Axes of the slice: x: 2, y: 2, z: 4, core: 2. Of those that a mesh axis runs over, the one named last changes fastest.
Arguments:
- tokens: bfloat16 [2048, 7168], P(('rep', 'node', 'local')), parts along dimension 0, may hold values from -6 to 6
- gate_ids: int32 [2048, 4], P(('rep', 'node', 'local')), parts along dimension 0, may hold values from 0 to 7, all different within a row; in each aligned block of 64 rows (0 to 63, 64 to 127, ...) at most 64 rows name the same one
- gate_values: bfloat16 [2048, 4], P(('rep', 'node', 'local')), parts along dimension 0, may hold values from 0.049804688 to 1
- w_gate: bfloat16 [8, 7168, 1024], P('node', None, 'local'), may hold values from -0.0625 to 0.0625
- w_up: bfloat16 [8, 7168, 1024], P('node', None, 'local'), may hold values from -0.0625 to 0.0625
- w_down: bfloat16 [8, 1024, 7168], P('node', 'local'), may hold values from -0.1875 to 0.1875
Outputs:
- mixed: bfloat16 [2048, 7168], P(('rep', 'node', 'local')), parts along dimension 0
The draws below stay inside these ranges and needn't reach their ends.
There are 2 independent parts, one for each index of `rep`. The reference program is written for one: setup_inputs(seed, part) draws one part's arguments, and reference() takes and returns one part's arrays. A program takes and returns all parts, laid end to end along the dimension named above; an argument that names none is the same for every part. Nothing has to cross between parts.
Inputs may be any that keep to these rules, and one draw needn't show every extreme that they name: `gate_ids`: each row names 4 different experts. Within the rows of one device, no expert is named by more than 64 rows, and in every draw some expert is named by exactly 64 rows of some device.
All inputs are finite; a program needn't handle non-finite values.
Results may differ from the reference program's by a relative error of at most 0.0065.
Values may be sent and summed in bfloat16 or wider, within the bound.
No kernel may reach another device: no remote copies, remote signals or barrier semaphores. Data moves between devices by JAX's collectives and lax.ppermute only.
A program may use at most 128 MiB of HBM per device.

```python
import math
import jax
import jax.numpy as jnp
import numpy as np
from jax import lax

D = 7168
HID = 1024
TOPK = 4
TOK_DEV = 64
EXPERTS = 8
CAP = 64
TOKENS = 1024
N_NODE = 8
N_LOCAL = 2


def block_levels(own_key, dims, shards, least, high):
    level, own = 1.0, jax.random.fold_in(own_key, 6)
    for axis_at, shards_of in shards:
        steps = jnp.exp(jax.random.uniform(jax.random.fold_in(own, axis_at), (shards_of,), jnp.float32, least / len(shards), high / len(shards)))
        level = level * jnp.repeat(steps, dims[axis_at] // shards_of).reshape([-1 if axis == axis_at else 1 for axis in range(len(dims))])
    return level


def shared_out(own_key, own, number, rows, amount, top, limit, lean):
    order = jax.random.permutation(own_key, amount)
    crowded, common = shares(amount, rows * top, limit, lean, True), shares(amount, rows * top, limit, lean, False)
    places = jnp.arange(amount)

    def named(tallies, rotation):
        used = int((tallies > 0).sum())
        fixed = max(1, used // 4)
        moved = fixed + (places - fixed + rotation * (used - fixed)) % max(1, amount - fixed)
        return jnp.zeros((amount,), jnp.int32).at[order[jnp.where(places < fixed, places, moved)]].set(jnp.asarray(tallies, jnp.int32))

    tallies = jnp.where(number % 4 == 0, named(crowded, number // 4), named(common, number - number // 4 - 1))
    mixed = jax.random.permutation(jax.random.fold_in(own, 3), amount)
    source_of, receiver = mixed[0:amount // 2 * 2:2], mixed[1:amount // 2 * 2:2]
    slack = jnp.minimum(tallies[source_of] - 1, limit - tallies[receiver]) // 2
    slack = jnp.where((source_of == order[0]) | (receiver == order[0]) | (tallies[receiver] == 0), 0, jnp.maximum(slack, 0))
    moved = jax.random.randint(jax.random.fold_in(own, 4), (amount // 2,), 0, 1 << 20) % (slack + 1)
    tallies = tallies.at[source_of].add(-moved).at[receiver].add(moved)
    members = jnp.searchsorted(jnp.cumsum(tallies), jnp.arange(rows * top), side="right").astype(jnp.int32)
    listing = members.reshape(top, rows).T
    listing = listing[jax.random.permutation(jax.random.fold_in(own, 1), rows)]
    rotation = jax.random.randint(jax.random.fold_in(own, 2), (rows, 1), 0, top)
    return jnp.take_along_axis(listing, (jnp.arange(top)[None, :] + rotation) % top, axis=1)


def shares(number_of, total, reach, slope, full):
    weights = [(1 << 20) // math.isqrt(grade ** slope) + 1 for grade in range(1, number_of + 1)]
    largest = reach if full else min(reach, max(-(-total // number_of), total * weights[0] // sum(weights)))
    least = 1 if total - largest >= number_of - 1 else 0
    given, surplus = [largest] + [least] * (number_of - 1), total - largest - least * (number_of - 1)
    while surplus > 0:
        movable = [i for i in range(1, number_of) if given[i] < largest] or [i for i in range(1, number_of) if given[i] < reach]
        pool, left = sum([weights[i] for i in movable]), surplus
        for i in movable:
            addition = min(reach - given[i], max(1, left * weights[i] // pool), surplus)
            given[i] = given[i] + addition
            surplus = surplus - addition
    return np.array(given)


def normal_values(own_key, shape, scale, reach, shards=(), kind=jnp.bfloat16):
    factor_of = block_levels(own_key, shape, shards, -0.22, 0.18) if shards else 1.0
    array = jax.random.normal(own_key, shape, jnp.float32) * scale * factor_of
    return jnp.minimum(jnp.maximum(array, -reach), reach).astype(kind)


def setup_inputs(seed: int = 0, part: int = 0) -> dict:
    splits = jax.random.split(jax.random.key(seed), 7)
    part_splits = jax.random.split(jax.random.fold_in(splits[6], part), 7)
    tokens = normal_values(part_splits[0], (TOKENS, D), 1.0, 6.0, ((0, 16),))
    gate_ids_keys = jax.random.split(jax.random.fold_in(part_splits[1], 1), TOKENS // TOK_DEV)
    gate_ids_turns = jax.random.permutation(jax.random.fold_in(part_splits[1], 3), TOKENS // TOK_DEV)
    gate_ids = jax.vmap(lambda own, number: shared_out(jax.random.fold_in(part_splits[1], 2), own, number, TOK_DEV, EXPERTS, TOPK, CAP, 2))(gate_ids_keys, gate_ids_turns).reshape((TOKENS, TOPK))
    gate_values = jnp.clip(jnp.exp(math.log(1.0) - 2.9996462 * jax.random.uniform(part_splits[2], (TOKENS, TOPK), jnp.float32) ** block_levels(part_splits[2], (TOKENS, TOPK), ((0, 16),), -0.2, 0.2)), 0.049804688, 1.0).astype(jnp.bfloat16)
    w_gate = normal_values(splits[3], (EXPERTS, D, HID), D ** -0.5, 0.0625, ((0, 8), (2, 2)))
    w_up = normal_values(splits[4], (EXPERTS, D, HID), D ** -0.5, 0.0625, ((0, 8), (2, 2)))
    w_down = normal_values(splits[5], (EXPERTS, HID, D), HID ** -0.5, 0.1875, ((0, 8), (1, 2)))
    return {"tokens": tokens, "gate_ids": gate_ids, "gate_values": gate_values, "w_gate": w_gate, "w_up": w_up, "w_down": w_down}


def slot_tables(gate_ids, gate_values):
    flat_ids = gate_ids.reshape(-1).astype(jnp.int32)
    expert_row = jnp.arange(EXPERTS, dtype=jnp.int32)
    onehot = (flat_ids[:, None] == expert_row[None, :]).astype(jnp.int32)
    earlier = jnp.cumsum(onehot, axis=0) - onehot
    within = jnp.sum(earlier * onehot, axis=1).astype(jnp.int32)
    slot = (flat_ids * CAP + within).reshape(TOK_DEV, TOPK)
    slot_row = jnp.arange(EXPERTS * CAP, dtype=jnp.int32)
    matches = slot[:, :, None] == slot_row[None, None, :]
    select = jnp.any(matches, axis=1).astype(jnp.bfloat16)
    combine_table = jnp.sum(jnp.where(matches, gate_values.astype(jnp.float32)[:, :, None], jnp.float32(0.0)), axis=1).astype(jnp.bfloat16)
    return select, combine_table


def expert_rows(args):
    rows, gate_mat, up_mat, down_mat = args
    gate_act = jnp.dot(rows, gate_mat, preferred_element_type=jnp.float32)
    up_act = jnp.dot(rows, up_mat, preferred_element_type=jnp.float32)
    hidden = (jax.nn.silu(gate_act) * up_act).astype(jnp.bfloat16)
    group = HID // N_LOCAL
    summed = jnp.zeros((rows.shape[0], D), jnp.float32)
    for part_index in range(N_LOCAL):
        piece = jnp.dot(hidden[:, part_index * group:(part_index + 1) * group], down_mat[part_index * group:(part_index + 1) * group], preferred_element_type=jnp.float32).astype(jnp.bfloat16)
        piece = lax.optimization_barrier(piece)
        summed = summed + piece.astype(jnp.float32)
    return summed.astype(jnp.bfloat16)


def reference(tokens, gate_ids, gate_values, w_gate, w_up, w_down):
    devices = N_NODE * N_LOCAL
    token_blocks = tokens.reshape(devices, TOK_DEV, D)
    select, combine_table = jax.vmap(slot_tables)(gate_ids.reshape(devices, TOK_DEV, TOPK), gate_values.reshape(devices, TOK_DEV, TOPK))
    dispatched = jnp.einsum("nts,ntd->nsd", select.astype(jnp.float32), token_blocks.astype(jnp.float32), precision=lax.Precision.HIGHEST).astype(jnp.bfloat16)
    by_expert = dispatched.reshape(devices, EXPERTS, CAP, D).transpose(1, 0, 2, 3).reshape(EXPERTS, devices * CAP, D)
    expert_out = lax.map(expert_rows, (by_expert, w_gate, w_up, w_down))
    back = expert_out.reshape(EXPERTS, devices, CAP, D).transpose(1, 0, 2, 3).reshape(devices, EXPERTS * CAP, D)
    mixed = jnp.einsum("nts,nsd->ntd", combine_table.astype(jnp.float32), back.astype(jnp.float32), precision=lax.Precision.HIGHEST)
    return mixed.astype(jnp.bfloat16).reshape(TOKENS, D)
```

```python
import functools

import jax
import jax.numpy as jnp
from jax import lax
from jax.experimental import pallas as pl
from jax.experimental.pallas import tpu as pltpu
from jax.sharding import PartitionSpec as P


def divisor_tile(extent, most, unit):
    best = unit
    for tile in range(unit, most + 1, unit):
        if extent % tile == 0:
            best = tile
    return best


def expert_kernel(count, hidden_steps, hidden_tile, *refs):
    rows_in = refs[:count]
    scale, gate_own, up_own, gate_other, up_other, down_own, down_other = refs[count : count + 7]
    rows_out = refs[count + 7 : 2 * count + 7]
    rows, hidden, arrived = refs[2 * count + 7 :]
    step = pl.program_id(0)
    height = rows_in[0].shape[0]
    half = hidden_steps // 2

    @pl.when(step == 0)
    def load():
        copies = [
            pltpu.make_async_copy(source, rows.at[pl.ds(i * height, height)], arrived.at[i])
            for i, source in enumerate(rows_in)
        ]
        for copy in copies:
            copy.start()
        for copy in copies:
            copy.wait()

    def project(gate, up):
        gate_act = jnp.dot(rows[...], gate[...], preferred_element_type=jnp.float32)
        up_act = jnp.dot(rows[...], up[...], preferred_element_type=jnp.float32)
        value = gate_act / (1.0 + jnp.exp(-gate_act)) * up_act
        hidden[step] = value.astype(jnp.bfloat16)

    @pl.when(step < half)
    def own():
        project(gate_own, up_own)

    @pl.when((step >= half) & (step < hidden_steps))
    def other():
        project(gate_other, up_other)

    @pl.when(step >= hidden_steps)
    def down():
        total = jnp.zeros((rows.shape[0], down_own.shape[1]), jnp.float32)
        for j in range(hidden_steps):
            source = down_own if j < half else down_other
            piece = source[(j % half) * hidden_tile : (j % half + 1) * hidden_tile, :]
            total += jnp.dot(hidden[j], piece, preferred_element_type=jnp.float32)
        total = total * scale[...]
        for i in range(count):
            rows_out[i][...] = total[i * height : (i + 1) * height].astype(jnp.bfloat16)


def expert_rows(blocks, scale, weights):
    count = len(blocks)
    height, width = blocks[0].shape
    depth = weights[0].shape[1]
    hidden_tile = divisor_tile(depth, 256, 128)
    half = depth // hidden_tile
    hidden_steps = 2 * half
    out_tile = divisor_tile(width, 1024, 128)
    out_steps = width // out_tile
    row_count = count * height

    def own_map(j):
        return (0, jnp.minimum(j, half - 1))

    def other_map(j):
        return (0, jnp.clip(j - half, 0, half - 1))

    def out_map(j):
        return (0, jnp.maximum(j - hidden_steps, 0))

    in_specs = (
        [pl.BlockSpec(memory_space=pl.ANY)] * count
        + [pl.BlockSpec((row_count, 1), lambda j: (0, 0))]
        + [pl.BlockSpec((width, hidden_tile), own_map)] * 2
        + [pl.BlockSpec((width, hidden_tile), other_map)] * 2
        + [pl.BlockSpec((depth, out_tile), out_map)] * 2
    )
    flops = 2 * row_count * width * depth * 6
    return pl.pallas_call(
        functools.partial(expert_kernel, count, hidden_steps, hidden_tile),
        grid=(hidden_steps + out_steps,),
        in_specs=in_specs,
        out_specs=[pl.BlockSpec((height, out_tile), out_map)] * count,
        out_shape=[jax.ShapeDtypeStruct((height, width), jnp.bfloat16)] * count,
        scratch_shapes=[
            pltpu.VMEM((row_count, width), jnp.bfloat16),
            pltpu.VMEM((hidden_steps, row_count, hidden_tile), jnp.bfloat16),
            pltpu.SemaphoreType.DMA((count,)),
        ],
        compiler_params=pltpu.CompilerParams(vmem_limit_bytes=48 * 1024 * 1024),
        cost_estimate=pl.CostEstimate(
            flops=flops,
            bytes_accessed=2 * (6 * width * depth + 2 * row_count * width),
            transcendentals=row_count * 2 * depth,
        ),
    )(*blocks, scale, *weights)


def per_device(tokens, gate_ids, gate_values, w_gate, w_up, w_down):
    nodes = lax.axis_size("node")
    node = lax.axis_index("node")

    def cross(array, step):
        return lax.ppermute(array, "node", [(n, n ^ step) for n in range(nodes)])

    def swap(array):
        return lax.ppermute(array, "local", [(0, 1), (1, 0)])

    blocks = {0: tokens}
    for step in range(2, nodes, 2):
        blocks[step] = cross(tokens, step)
    for step in range(0, nodes, 2):
        blocks[step + 1] = cross(blocks[step], 1)

    own = [w_gate[0], w_up[0], w_down[0]]
    other = [swap(w) for w in own]
    weights = [own[0], own[1], other[0], other[1], own[2], other[2]]

    experts = jnp.arange(nodes, dtype=jnp.int32)
    chosen = gate_ids[:, :, None] == experts[None, None, :]
    table = jnp.sum(
        jnp.where(chosen, gate_values.astype(jnp.float32)[:, :, None], 0.0), axis=1
    ).astype(jnp.bfloat16)
    tables = lax.all_gather(table, "node", axis=0)
    mine = jnp.sum(
        jnp.where(experts == node, tables.astype(jnp.float32), 0.0), axis=2
    )
    source = (node ^ experts)[:, None] == experts[None, :]
    scales = jnp.sum(jnp.where(source[:, :, None], mine[None], 0.0), axis=1)

    group = min(nodes, 4)
    shares = {}
    for first in range(0, nodes, group):
        steps = range(first, first + group)
        scale = scales[first : first + group].reshape(-1, 1)
        results = expert_rows([blocks[s] for s in steps], scale, weights)
        shares.update(zip(steps, results))

    total = None
    for step in range(0, nodes, 2):
        part = shares[step].astype(jnp.float32) + cross(shares[step + 1], 1).astype(jnp.float32)
        if step:
            part = cross(part.astype(jnp.bfloat16), step).astype(jnp.float32)
        total = part if total is None else total + part
    return total.astype(jnp.bfloat16)


def solution(mesh):
    return jax.shard_map(
        per_device,
        mesh=mesh,
        in_specs=(
            P(("rep", "node", "local"), None),
            P(("rep", "node", "local"), None),
            P(("rep", "node", "local"), None),
            P("node", None, "local"),
            P("node", None, "local"),
            P("node", "local", None),
        ),
        out_specs=P(("rep", "node", "local"), None),
        check_vma=False,
    )
```

```python
import functools

import jax
import jax.numpy as jnp
from jax import lax
from jax.experimental import pallas as pl
from jax.experimental.pallas import tpu as pltpu
from jax.sharding import PartitionSpec as P

LANES = 128
RING = 4
KERNEL_VMEM = 54 * 1024 * 1024


def divisor_tile(extent, most, unit):
    best = unit
    for tile in range(unit, most + 1, unit):
        if extent % tile == 0:
            best = tile
    return best


def expert_kernel(count, slab, out_tile, *refs):
    blocks = refs[:count]
    node, gate_own, up_own, gate_other, up_other, down_own, down_other = refs[count : count + 7]
    results = refs[count + 7 : 2 * count + 7]
    rows, gates, ups, downs, gate_sum, up_sum, hidden, staged = refs[2 * count + 7 : 2 * count + 15]
    block_sem, gate_sem, up_sem, down_sem, out_sem = refs[2 * count + 15 :]
    height = blocks[0].shape[0]
    _, width, depth = gate_own.shape
    slabs = width // slab
    tiles = width // out_tile

    def block_copy(i):
        return pltpu.make_async_copy(
            blocks[i], rows.at[pl.ds(i * height, height)], block_sem.at[i]
        )

    def slab_copies(gate, up, index, slot):
        place = pl.ds(pl.multiple_of(index * slab, slab), slab)
        return (
            pltpu.make_async_copy(gate.at[0, place], gates.at[slot], gate_sem.at[slot]),
            pltpu.make_async_copy(up.at[0, place], ups.at[slot], up_sem.at[slot]),
        )

    def down_copies(tile):
        slot = lax.rem(tile, RING)
        place = pl.ds(pl.multiple_of(tile * out_tile, out_tile), out_tile)
        return (
            pltpu.make_async_copy(down_own.at[0, :, place], downs.at[slot, 0], down_sem.at[slot, 0]),
            pltpu.make_async_copy(down_other.at[0, :, place], downs.at[slot, 1], down_sem.at[slot, 1]),
        )

    def start_load(index):
        slot = lax.rem(index, RING)

        @pl.when(index < slabs)
        def own():
            for copy in slab_copies(gate_own, up_own, index, slot):
                copy.start()

        @pl.when((index >= slabs) & (index < 2 * slabs))
        def other():
            for copy in slab_copies(gate_other, up_other, index - slabs, slot):
                copy.start()

        @pl.when((index >= 2 * slabs) & (index < 2 * slabs + tiles))
        def down():
            for copy in down_copies(index - 2 * slabs):
                copy.start()

    def out_copies(tile, slot):
        place = pl.ds(pl.multiple_of(tile * out_tile, out_tile), out_tile)
        return [
            pltpu.make_async_copy(
                staged.at[slot, pl.ds(i * height, height)],
                results[i].at[:, place],
                out_sem.at[slot, i],
            )
            for i in range(count)
        ]

    for i in range(count):
        block_copy(i).start()
    for index in range(RING):
        start_load(jnp.int32(index))
    for i in range(count):
        block_copy(i).wait()

    def project(index, half):
        slot = lax.rem(index, RING)
        local = index - half * slabs
        for copy in slab_copies(gate_own, up_own, local, slot):
            copy.wait()
        piece = rows[:, pl.ds(pl.multiple_of(local * slab, slab), slab)]
        gate_part = jnp.dot(piece, gates[slot], preferred_element_type=jnp.float32)
        up_part = jnp.dot(piece, ups[slot], preferred_element_type=jnp.float32)

        @pl.when(local == 0)
        def first():
            gate_sum[...] = gate_part
            up_sum[...] = up_part

        @pl.when(local > 0)
        def later():
            gate_sum[...] += gate_part
            up_sum[...] += up_part

        start_load(index + RING)

    for half in range(2):
        lax.fori_loop(
            half * slabs, (half + 1) * slabs, lambda i, _, half=half: project(i, half), None
        )
        act = gate_sum[...]
        hidden[half] = (act / (1.0 + jnp.exp(-act)) * up_sum[...]).astype(jnp.bfloat16)

    table = rows[:, width:].astype(jnp.float32)
    lane = lax.broadcasted_iota(jnp.int32, table.shape, 1)
    scale = jnp.sum(jnp.where(lane == node[0], table, 0.0), axis=1, keepdims=True)

    def down(tile, _):
        slot = lax.rem(tile, RING)
        out_slot = lax.rem(tile, 2)
        for copy in down_copies(tile):
            copy.wait()
        total = jnp.dot(hidden[0], downs[slot, 0], preferred_element_type=jnp.float32)
        total += jnp.dot(hidden[1], downs[slot, 1], preferred_element_type=jnp.float32)
        start_load(2 * slabs + tile + RING)

        @pl.when(tile >= 2)
        def free():
            for copy in out_copies(tile - 2, out_slot):
                copy.wait()

        staged[out_slot] = (total * scale).astype(jnp.bfloat16)
        for copy in out_copies(tile, out_slot):
            copy.start()

    lax.fori_loop(0, tiles, down, None)
    for tile in range(max(0, tiles - 2), tiles):
        for copy in out_copies(tile, tile % 2):
            copy.wait()


def expert_rows(blocks, node, weights):
    count = len(blocks)
    height, total_width = blocks[0].shape
    _, width, depth = weights[0].shape
    slab = divisor_tile(width, 1024, 128)
    out_tile = divisor_tile(width, 1024, 128)
    tiles = width // out_tile
    row_count = count * height
    anywhere = pl.BlockSpec(memory_space=pl.ANY)
    return pl.pallas_call(
        functools.partial(expert_kernel, count, slab, out_tile),
        in_specs=[anywhere] * count
        + [pl.BlockSpec(memory_space=pltpu.SMEM)]
        + [pl.BlockSpec(memory_space=pltpu.HBM)] * 6,
        out_specs=[anywhere] * count,
        out_shape=[jax.ShapeDtypeStruct((height, width), jnp.bfloat16)] * count,
        scratch_shapes=[
            pltpu.VMEM((row_count, total_width), jnp.bfloat16),
            pltpu.VMEM((RING, slab, depth), jnp.bfloat16),
            pltpu.VMEM((RING, slab, depth), jnp.bfloat16),
            pltpu.VMEM((RING, 2, depth, out_tile), jnp.bfloat16),
            pltpu.VMEM((row_count, depth), jnp.float32),
            pltpu.VMEM((row_count, depth), jnp.float32),
            pltpu.VMEM((2, row_count, depth), jnp.bfloat16),
            pltpu.VMEM((2, row_count, out_tile), jnp.bfloat16),
            pltpu.SemaphoreType.DMA((count,)),
            pltpu.SemaphoreType.DMA((RING,)),
            pltpu.SemaphoreType.DMA((RING,)),
            pltpu.SemaphoreType.DMA((RING, 2)),
            pltpu.SemaphoreType.DMA((2, count)),
        ],
        compiler_params=pltpu.CompilerParams(vmem_limit_bytes=KERNEL_VMEM),
        cost_estimate=pl.CostEstimate(
            flops=12 * row_count * width * depth,
            bytes_accessed=2 * (6 * width * depth + 2 * row_count * width),
            transcendentals=2 * row_count * depth,
        ),
    )(*blocks, node, *weights)


def joined(*arrays):
    return lax.optimization_barrier(arrays)


def plus(*arrays):
    total = arrays[0].astype(jnp.float32)
    for array in arrays[1:]:
        total = total + array.astype(jnp.float32)
    return total.astype(jnp.bfloat16)


def per_device(tokens, gate_ids, gate_values, w_gate, w_up, w_down):
    nodes = lax.axis_size("node")
    node = lax.axis_index("node")

    def send(array, pairs):
        return lax.ppermute(array, "node", pairs)

    def cross(array, step):
        return send(array, [(n, n ^ step) for n in range(nodes)])

    def swap(array):
        return lax.ppermute(array, "local", [(0, 1), (1, 0)])

    lanes = jnp.arange(LANES, dtype=jnp.int32)
    chosen = gate_ids[:, :, None] == lanes[None, None, :]
    table = jnp.sum(
        jnp.where(chosen, gate_values.astype(jnp.float32)[:, :, None], 0.0), axis=1
    ).astype(jnp.bfloat16)
    mine = jnp.concatenate([tokens, table], axis=1)

    place = node.astype(jnp.int32).reshape(1)

    def experts(others, *blocks):
        weights = [w_gate, w_up, others[0], others[1], w_down, others[2]]
        return expert_rows(blocks, place, weights)

    halves = (w_gate, w_up, w_down)
    if nodes == 8:
        return line_plan(mine, node, send, cross, swap, halves, experts)
    others = [swap(half) for half in halves]
    return direct_plan(mine, nodes, cross, functools.partial(experts, others))


def line_plan(mine, node, send, cross, swap, halves, experts):
    middle = [(2, 4), (4, 2), (3, 5), (5, 3)]
    outward = [(2, 0), (3, 1), (4, 6), (5, 7)]
    inward = [(b, a) for a, b in outward]
    inner = (node >= 2) & (node < 6)

    s0, (w_gate, w_up, w_down) = mine, halves
    s1, m2, t0, v_gate, w_up, w_down = joined(
        cross(s0, 2), send(s0, middle), cross(s0, 1), swap(w_gate), w_up, w_down
    )
    e2, m3, t1, v_up, v_down = joined(
        send(m2, outward), send(s1, middle), cross(s1, 1), swap(w_up), swap(w_down)
    )
    experts = functools.partial(experts, (v_gate, v_up, v_down))
    s2 = jnp.where(inner, m2, e2)
    e3, t2, p0, q0, p1, q1 = joined(send(m3, outward), cross(s2, 1), *experts(s0, t0, s1, t1))
    s3 = jnp.where(inner, m3, e3)
    t3, p2, q2, p3 = joined(cross(s3, 1), *experts(s2, t2, s3))
    q3, y2 = joined(*experts(t3), cross(q2, 1))

    p2 = plus(p2, y2)
    y3, i2 = joined(cross(q3, 1), send(p2, inward))
    p3, p2 = plus(p3, y3), plus(p2, i2)
    i3, f2, y1 = joined(send(p3, inward), send(p2, middle), cross(q1, 1))
    p3, p1 = plus(p3, i3), plus(p1, y1)
    i1, y0 = joined(send(p3, middle), cross(q0, 1))
    p1 = plus(p1, i1)
    return plus(p0, y0, cross(p1, 2), f2)


def direct_plan(mine, nodes, cross, experts):
    blocks = {0: mine}
    for step in range(2, nodes, 2):
        blocks[step] = cross(mine, step)
    for step in range(0, nodes, 2):
        blocks[step + 1] = cross(blocks[step], 1)
    shares = {}
    group = min(nodes, 4)
    for first in range(0, nodes, group):
        steps = range(first, first + group)
        shares.update(zip(steps, experts(*[blocks[s] for s in steps])))
    sums = []
    for step in range(0, nodes, 2):
        part = plus(shares[step], cross(shares[step + 1], 1))
        sums.append(cross(part, step) if step else part)
    return plus(*sums)


def solution(mesh):
    return jax.shard_map(
        per_device,
        mesh=mesh,
        in_specs=(
            P(("rep", "node", "local"), None),
            P(("rep", "node", "local"), None),
            P(("rep", "node", "local"), None),
            P("node", None, "local"),
            P("node", None, "local"),
            P("node", "local", None),
        ),
        out_specs=P(("rep", "node", "local"), None),
        check_vma=False,
    )
```

```python
import functools

import jax
import jax.numpy as jnp
from jax import lax
from jax.experimental import pallas as pl
from jax.experimental.pallas import tpu as pltpu
from jax.sharding import PartitionSpec as P

LANES = 128
RING = 3
KERNEL_VMEM = 54 * 1024 * 1024


def divisor_tile(extent, most, unit):
    best = unit
    for tile in range(unit, most + 1, unit):
        if extent % tile == 0:
            best = tile
    return best


def expert_kernel(count, slab, out_tile, *refs):
    blocks = refs[:count]
    node, gate_own, up_own, gate_other, up_other, down_own, down_other = refs[count : count + 7]
    results = refs[count + 7 : 2 * count + 7]
    rows, gates, ups, downs, gate_sum, up_sum, hidden, staged = refs[2 * count + 7 : 2 * count + 15]
    block_sem, gate_sem, up_sem, down_sem, out_sem = refs[2 * count + 15 :]
    heights = [block.shape[0] for block in blocks]
    starts = [sum(heights[:i]) for i in range(count)]
    _, width, depth = gate_own.shape
    slabs = width // slab
    tiles = width // out_tile

    def block_copy(i):
        return pltpu.make_async_copy(
            blocks[i], rows.at[pl.ds(starts[i], heights[i])], block_sem.at[i]
        )

    def slab_copies(gate, up, index, slot):
        place = pl.ds(pl.multiple_of(index * slab, slab), slab)
        return (
            pltpu.make_async_copy(gate.at[0, place], gates.at[slot], gate_sem.at[slot]),
            pltpu.make_async_copy(up.at[0, place], ups.at[slot], up_sem.at[slot]),
        )

    def down_copies(tile):
        slot = lax.rem(tile, RING)
        place = pl.ds(pl.multiple_of(tile * out_tile, out_tile), out_tile)
        return (
            pltpu.make_async_copy(down_own.at[0, :, place], downs.at[slot, 0], down_sem.at[slot, 0]),
            pltpu.make_async_copy(down_other.at[0, :, place], downs.at[slot, 1], down_sem.at[slot, 1]),
        )

    def start_load(index):
        slot = lax.rem(index, RING)

        @pl.when(index < slabs)
        def own():
            for copy in slab_copies(gate_own, up_own, index, slot):
                copy.start()

        @pl.when((index >= slabs) & (index < 2 * slabs))
        def other():
            for copy in slab_copies(gate_other, up_other, index - slabs, slot):
                copy.start()

        @pl.when((index >= 2 * slabs) & (index < 2 * slabs + tiles))
        def down():
            for copy in down_copies(index - 2 * slabs):
                copy.start()

    def out_copies(tile, slot):
        place = pl.ds(pl.multiple_of(tile * out_tile, out_tile), out_tile)
        return [
            pltpu.make_async_copy(
                staged.at[slot, pl.ds(starts[i], heights[i])],
                results[i].at[:, place],
                out_sem.at[slot, i],
            )
            for i in range(count)
        ]

    for i in range(count):
        block_copy(i).start()
    for index in range(RING):
        start_load(jnp.int32(index))
    for i in range(count):
        block_copy(i).wait()

    def project(index, half):
        slot = lax.rem(index, RING)
        local = index - half * slabs
        for copy in slab_copies(gate_own, up_own, local, slot):
            copy.wait()
        piece = rows[:, pl.ds(pl.multiple_of(local * slab, slab), slab)]
        gate_part = jnp.dot(piece, gates[slot], preferred_element_type=jnp.float32)
        up_part = jnp.dot(piece, ups[slot], preferred_element_type=jnp.float32)

        @pl.when(local == 0)
        def first():
            gate_sum[...] = gate_part
            up_sum[...] = up_part

        @pl.when(local > 0)
        def later():
            gate_sum[...] += gate_part
            up_sum[...] += up_part

        start_load(index + RING)

    for half in range(2):
        lax.fori_loop(
            half * slabs, (half + 1) * slabs, lambda i, _, half=half: project(i, half), None
        )
        act = gate_sum[...]
        hidden[half] = (act / (1.0 + jnp.exp(-act)) * up_sum[...]).astype(jnp.bfloat16)

    table = rows[:, width:].astype(jnp.float32)
    lane = lax.broadcasted_iota(jnp.int32, table.shape, 1)
    scale = jnp.sum(jnp.where(lane == node[0], table, 0.0), axis=1, keepdims=True)

    def down(tile, _):
        slot = lax.rem(tile, RING)
        out_slot = lax.rem(tile, 2)
        for copy in down_copies(tile):
            copy.wait()
        total = jnp.dot(hidden[0], downs[slot, 0], preferred_element_type=jnp.float32)
        total += jnp.dot(hidden[1], downs[slot, 1], preferred_element_type=jnp.float32)
        start_load(2 * slabs + tile + RING)

        @pl.when(tile >= 2)
        def free():
            for copy in out_copies(tile - 2, out_slot):
                copy.wait()

        staged[out_slot] = (total * scale).astype(jnp.bfloat16)
        for copy in out_copies(tile, out_slot):
            copy.start()

    lax.fori_loop(0, tiles, down, None)
    for tile in range(max(0, tiles - 2), tiles):
        for copy in out_copies(tile, tile % 2):
            copy.wait()


def expert_rows(blocks, node, weights):
    count = len(blocks)
    total_width = blocks[0].shape[1]
    _, width, depth = weights[0].shape
    slab = divisor_tile(width, 1792, 128)
    out_tile = divisor_tile(width, 1024, 128)
    tiles = width // out_tile
    row_count = sum(block.shape[0] for block in blocks)
    anywhere = pl.BlockSpec(memory_space=pl.ANY)
    return pl.pallas_call(
        functools.partial(expert_kernel, count, slab, out_tile),
        in_specs=[anywhere] * count
        + [pl.BlockSpec(memory_space=pltpu.SMEM)]
        + [pl.BlockSpec(memory_space=pltpu.HBM)] * 6,
        out_specs=[anywhere] * count,
        out_shape=[jax.ShapeDtypeStruct((block.shape[0], width), jnp.bfloat16) for block in blocks],
        scratch_shapes=[
            pltpu.VMEM((row_count, total_width), jnp.bfloat16),
            pltpu.VMEM((RING, slab, depth), jnp.bfloat16),
            pltpu.VMEM((RING, slab, depth), jnp.bfloat16),
            pltpu.VMEM((RING, 2, depth, out_tile), jnp.bfloat16),
            pltpu.VMEM((row_count, depth), jnp.float32),
            pltpu.VMEM((row_count, depth), jnp.float32),
            pltpu.VMEM((2, row_count, depth), jnp.bfloat16),
            pltpu.VMEM((2, row_count, out_tile), jnp.bfloat16),
            pltpu.SemaphoreType.DMA((count,)),
            pltpu.SemaphoreType.DMA((RING,)),
            pltpu.SemaphoreType.DMA((RING,)),
            pltpu.SemaphoreType.DMA((RING, 2)),
            pltpu.SemaphoreType.DMA((2, count)),
        ],
        compiler_params=pltpu.CompilerParams(vmem_limit_bytes=KERNEL_VMEM),
        cost_estimate=pl.CostEstimate(
            flops=12 * row_count * width * depth,
            bytes_accessed=2 * (6 * width * depth + 2 * row_count * width),
            transcendentals=2 * row_count * depth,
        ),
    )(*blocks, node, *weights)


def joined(*arrays):
    return lax.optimization_barrier(arrays)


def plus(*arrays):
    total = arrays[0].astype(jnp.float32)
    for array in arrays[1:]:
        total = total + array.astype(jnp.float32)
    return total.astype(jnp.bfloat16)


def per_device(tokens, gate_ids, gate_values, w_gate, w_up, w_down):
    nodes = lax.axis_size("node")
    node = lax.axis_index("node")

    def send(array, pairs):
        return lax.ppermute(array, "node", pairs)

    def cross(array, step):
        return send(array, [(n, n ^ step) for n in range(nodes)])

    def swap(array):
        return lax.ppermute(array, "local", [(0, 1), (1, 0)])

    lanes = jnp.arange(LANES, dtype=jnp.int32)
    chosen = gate_ids[:, :, None] == lanes[None, None, :]
    table = jnp.sum(
        jnp.where(chosen, gate_values.astype(jnp.float32)[:, :, None], 0.0), axis=1
    ).astype(jnp.bfloat16)
    mine = jnp.concatenate([tokens, table], axis=1)

    place = node.astype(jnp.int32).reshape(1)

    def experts(others, *blocks):
        weights = [w_gate, w_up, others[0], others[1], w_down, others[2]]
        return expert_rows(blocks, place, weights)

    halves = (w_gate, w_up, w_down)
    if nodes == 8:
        return line_plan(mine, node, send, cross, swap, halves, experts)
    others = [swap(half) for half in halves]
    return direct_plan(mine, nodes, cross, functools.partial(experts, others))


def line_plan(mine, node, send, cross, swap, halves, experts):
    middle = [(2, 4), (4, 2), (3, 5), (5, 3)]
    outward = [(2, 0), (3, 1), (4, 6), (5, 7)]
    inward = [(b, a) for a, b in outward]
    inner = (node >= 2) & (node < 6)

    s0, (w_gate, w_up, w_down) = mine, halves
    cut = mine.shape[0] // 2
    v_gate, v_up = swap(w_gate), swap(w_up)
    s1, m2, t0, w_down = joined(cross(s0, 2), send(s0, middle), cross(s0, 1), w_down)
    v_gate, w_down = joined(v_gate, w_down)
    e2, m3, t1, v_up, v_down = joined(
        send(m2, outward), send(s1, middle), cross(s1, 1), v_up, swap(w_down)
    )
    experts = functools.partial(experts, (v_gate, v_up, v_down))
    s2 = jnp.where(inner, m2, e2)
    e3, t2, n3, q1, p2 = joined(
        send(m3, outward), cross(s2, 1), send(t1[cut:], middle), *experts(t1, s2)
    )
    t3, o3, m3, e3 = joined(
        cross(jnp.where(inner, m3[:cut], e3[:cut]), 1), send(n3, outward), m3, e3
    )
    s3 = jnp.where(inner, m3, e3)
    q2, p3, q3, r3, s0, t0, s1 = joined(
        *experts(t2, s3, t3, jnp.where(inner, n3, o3)), s0, t0, s1
    )

    y3, v3 = joined(cross(q3, 1), send(r3, inward))
    p3, r3 = jnp.concatenate([plus(p3[:cut], y3), p3[cut:]]), plus(r3, v3)
    i3, y2, v1 = joined(send(p3, inward), cross(q2, 1), send(r3, middle))
    p3, p2, q1 = plus(p3, i3), plus(p2, y2), jnp.concatenate([q1[:cut], plus(q1[cut:], v1)])
    p3, p2, q1, s0, t0, s1 = joined(p3, p2, q1, s0, t0, s1)
    i1, i2, y1, p0, q0, p1 = joined(
        send(p3, middle), send(p2, inward), cross(q1, 1), *experts(s0, t0, s1)
    )
    p1, p2 = plus(p1, y1, i1), plus(p2, i2)
    return plus(p0, cross(q0, 1), cross(p1, 2), send(p2, middle))


def direct_plan(mine, nodes, cross, experts):
    blocks = {0: mine}
    for step in range(2, nodes, 2):
        blocks[step] = cross(mine, step)
    for step in range(0, nodes, 2):
        blocks[step + 1] = cross(blocks[step], 1)
    shares = {}
    group = min(nodes, 4)
    for first in range(0, nodes, group):
        steps = range(first, first + group)
        shares.update(zip(steps, experts(*[blocks[s] for s in steps])))
    sums = []
    for step in range(0, nodes, 2):
        part = plus(shares[step], cross(shares[step + 1], 1))
        sums.append(cross(part, step) if step else part)
    return plus(*sums)


def solution(mesh):
    return jax.shard_map(
        per_device,
        mesh=mesh,
        in_specs=(
            P(("rep", "node", "local"), None),
            P(("rep", "node", "local"), None),
            P(("rep", "node", "local"), None),
            P("node", None, "local"),
            P("node", None, "local"),
            P("node", "local", None),
        ),
        out_specs=P(("rep", "node", "local"), None),
        check_vma=False,
    )
```

```python
import functools

import jax
import jax.numpy as jnp
from jax import lax
from jax.experimental import pallas as pl
from jax.experimental.pallas import tpu as pltpu
from jax.sharding import PartitionSpec as P

LANES = 128
RING = 3
KERNEL_VMEM = 50 * 1024 * 1024


def divisor_tile(extent, most, unit):
    best = unit
    for tile in range(unit, most + 1, unit):
        if extent % tile == 0:
            best = tile
    return best


def expert_kernel(count, slab, out_tile, *refs):
    blocks = refs[:count]
    node, gate_own, up_own, gate_other, up_other, down_own, down_other = refs[count : count + 7]
    results = refs[count + 7 : 2 * count + 7]
    rows, gates, ups, downs, gate_sum, up_sum, hidden, staged = refs[2 * count + 7 : 2 * count + 15]
    block_sem, gate_sem, up_sem, down_sem, out_sem = refs[2 * count + 15 :]
    heights = [block.shape[0] for block in blocks]
    starts = [sum(heights[:i]) for i in range(count)]
    _, width, depth = gate_own.shape
    slabs = width // slab
    tiles = width // out_tile

    def block_copy(i):
        return pltpu.make_async_copy(
            blocks[i], rows.at[pl.ds(starts[i], heights[i])], block_sem.at[i]
        )

    def slab_copies(gate, up, index, slot):
        place = pl.ds(pl.multiple_of(index * slab, slab), slab)
        return (
            pltpu.make_async_copy(gate.at[0, place], gates.at[slot], gate_sem.at[slot]),
            pltpu.make_async_copy(up.at[0, place], ups.at[slot], up_sem.at[slot]),
        )

    def down_copies(tile):
        slot = lax.rem(tile, RING)
        place = pl.ds(pl.multiple_of(tile * out_tile, out_tile), out_tile)
        return (
            pltpu.make_async_copy(down_own.at[0, :, place], downs.at[slot, 0], down_sem.at[slot, 0]),
            pltpu.make_async_copy(down_other.at[0, :, place], downs.at[slot, 1], down_sem.at[slot, 1]),
        )

    def start_load(index):
        slot = lax.rem(index, RING)

        @pl.when(index < slabs)
        def own():
            for copy in slab_copies(gate_own, up_own, index, slot):
                copy.start()

        @pl.when((index >= slabs) & (index < 2 * slabs))
        def other():
            for copy in slab_copies(gate_other, up_other, index - slabs, slot):
                copy.start()

        @pl.when((index >= 2 * slabs) & (index < 2 * slabs + tiles))
        def down():
            for copy in down_copies(index - 2 * slabs):
                copy.start()

    def out_copies(tile, slot):
        place = pl.ds(pl.multiple_of(tile * out_tile, out_tile), out_tile)
        return [
            pltpu.make_async_copy(
                staged.at[slot, pl.ds(starts[i], heights[i])],
                results[i].at[:, place],
                out_sem.at[slot, i],
            )
            for i in range(count)
        ]

    for i in range(count):
        block_copy(i).start()
    for index in range(RING):
        start_load(jnp.int32(index))
    for i in range(count):
        block_copy(i).wait()

    def project(index, half):
        slot = lax.rem(index, RING)
        local = index - half * slabs
        for copy in slab_copies(gate_own, up_own, local, slot):
            copy.wait()
        piece = rows[:, pl.ds(pl.multiple_of(local * slab, slab), slab)]
        gate_part = jnp.dot(piece, gates[slot], preferred_element_type=jnp.float32)
        up_part = jnp.dot(piece, ups[slot], preferred_element_type=jnp.float32)

        @pl.when(local == 0)
        def first():
            gate_sum[...] = gate_part
            up_sum[...] = up_part

        @pl.when(local > 0)
        def later():
            gate_sum[...] += gate_part
            up_sum[...] += up_part

        start_load(index + RING)

    for half in range(2):
        lax.fori_loop(
            half * slabs, (half + 1) * slabs, lambda i, _, half=half: project(i, half), None
        )
        act = gate_sum[...]
        hidden[half] = (act / (1.0 + jnp.exp(-act)) * up_sum[...]).astype(jnp.bfloat16)

    table = rows[:, width:].astype(jnp.float32)
    lane = lax.broadcasted_iota(jnp.int32, table.shape, 1)
    scale = jnp.sum(jnp.where(lane == node[0], table, 0.0), axis=1, keepdims=True)

    def down(tile, _):
        slot = lax.rem(tile, RING)
        out_slot = lax.rem(tile, 2)
        for copy in down_copies(tile):
            copy.wait()
        total = jnp.dot(hidden[0], downs[slot, 0], preferred_element_type=jnp.float32)
        total += jnp.dot(hidden[1], downs[slot, 1], preferred_element_type=jnp.float32)
        start_load(2 * slabs + tile + RING)

        @pl.when(tile >= 2)
        def free():
            for copy in out_copies(tile - 2, out_slot):
                copy.wait()

        staged[out_slot] = (total * scale).astype(jnp.bfloat16)
        for copy in out_copies(tile, out_slot):
            copy.start()

    lax.fori_loop(0, tiles, down, None)
    for tile in range(max(0, tiles - 2), tiles):
        for copy in out_copies(tile, tile % 2):
            copy.wait()


def expert_rows(blocks, node, weights):
    count = len(blocks)
    total_width = blocks[0].shape[1]
    _, width, depth = weights[0].shape
    slab = divisor_tile(width, 1792, 128)
    out_tile = divisor_tile(width, 1024, 128)
    tiles = width // out_tile
    row_count = sum(block.shape[0] for block in blocks)
    anywhere = pl.BlockSpec(memory_space=pl.ANY)
    return pl.pallas_call(
        functools.partial(expert_kernel, count, slab, out_tile),
        in_specs=[anywhere] * count
        + [pl.BlockSpec(memory_space=pltpu.SMEM)]
        + [pl.BlockSpec(memory_space=pltpu.HBM)] * 6,
        out_specs=[anywhere] * count,
        out_shape=[jax.ShapeDtypeStruct((block.shape[0], width), jnp.bfloat16) for block in blocks],
        scratch_shapes=[
            pltpu.VMEM((row_count, total_width), jnp.bfloat16),
            pltpu.VMEM((RING, slab, depth), jnp.bfloat16),
            pltpu.VMEM((RING, slab, depth), jnp.bfloat16),
            pltpu.VMEM((RING, 2, depth, out_tile), jnp.bfloat16),
            pltpu.VMEM((row_count, depth), jnp.float32),
            pltpu.VMEM((row_count, depth), jnp.float32),
            pltpu.VMEM((2, row_count, depth), jnp.bfloat16),
            pltpu.VMEM((2, row_count, out_tile), jnp.bfloat16),
            pltpu.SemaphoreType.DMA((count,)),
            pltpu.SemaphoreType.DMA((RING,)),
            pltpu.SemaphoreType.DMA((RING,)),
            pltpu.SemaphoreType.DMA((RING, 2)),
            pltpu.SemaphoreType.DMA((2, count)),
        ],
        compiler_params=pltpu.CompilerParams(vmem_limit_bytes=KERNEL_VMEM),
        cost_estimate=pl.CostEstimate(
            flops=12 * row_count * width * depth,
            bytes_accessed=2 * (6 * width * depth + 2 * row_count * width),
            transcendentals=2 * row_count * depth,
        ),
    )(*blocks, node, *weights)


def joined(*arrays):
    return lax.optimization_barrier(arrays)


def plus(*arrays):
    total = arrays[0].astype(jnp.float32)
    for array in arrays[1:]:
        total = total + array.astype(jnp.float32)
    return total.astype(jnp.bfloat16)


def per_device(tokens, gate_ids, gate_values, w_gate, w_up, w_down):
    nodes = lax.axis_size("node")
    node = lax.axis_index("node")

    def send(array, pairs):
        return lax.ppermute(array, "node", pairs)

    def cross(array, step):
        return send(array, [(n, n ^ step) for n in range(nodes)])

    def swap(array):
        return lax.ppermute(array, "local", [(0, 1), (1, 0)])

    lanes = jnp.arange(LANES, dtype=jnp.int32)
    chosen = gate_ids[:, :, None] == lanes[None, None, :]
    table = jnp.sum(
        jnp.where(chosen, gate_values.astype(jnp.float32)[:, :, None], 0.0), axis=1
    ).astype(jnp.bfloat16)
    mine = jnp.concatenate([tokens, table], axis=1)

    place = node.astype(jnp.int32).reshape(1)

    def experts(others, *blocks):
        weights = [w_gate, w_up, others[0], others[1], w_down, others[2]]
        return expert_rows(blocks, place, weights)

    halves = (w_gate, w_up, w_down)
    if nodes == 8:
        return line_plan(mine, node, send, cross, swap, halves, experts)
    others = [swap(half) for half in halves]
    return direct_plan(mine, nodes, cross, functools.partial(experts, others))


def line_plan(mine, node, send, cross, swap, halves, experts):
    middle = [(2, 4), (4, 2), (3, 5), (5, 3)]
    outward = [(2, 0), (3, 1), (4, 6), (5, 7)]
    inward = [(b, a) for a, b in outward]
    inner = (node >= 2) & (node < 6)

    s0, (w_gate, w_up, w_down) = mine, halves
    cut = mine.shape[0] // 2
    v_gate, v_up = swap(w_gate), swap(w_up)
    s1, m2, t0, w_down = joined(cross(s0, 2), send(s0, middle), cross(s0, 1), w_down)
    v_gate, w_down = joined(v_gate, w_down)
    m3 = send(s1, middle)
    e2, t1, v_up, v_down = joined(send(m2, outward), cross(s1, 1), v_up, swap(w_down))
    experts = functools.partial(experts, (v_gate, v_up, v_down))
    s2 = jnp.where(inner, m2, e2)
    e3, t2, n3, q1, p2 = joined(
        send(m3, outward), cross(s2, 1), send(t1[cut:], middle), *experts(t1, s2)
    )
    t3, o3, m3, e3 = joined(
        cross(jnp.where(inner, m3[:cut], e3[:cut]), 1), send(n3, outward), m3, e3
    )
    s3 = jnp.where(inner, m3, e3)
    q2, p3, q3, r3, s0, t0, s1 = joined(
        *experts(t2, s3, t3, jnp.where(inner, n3, o3)), s0, t0, s1
    )

    y3, v3 = joined(cross(q3, 1), send(r3, inward))
    p3, r3 = jnp.concatenate([plus(p3[:cut], y3), p3[cut:]]), plus(r3, v3)
    i3, y2, v1 = joined(send(p3, inward), cross(q2, 1), send(r3, middle))
    p3, p2, q1 = plus(p3, i3), plus(p2, y2), jnp.concatenate([q1[:cut], plus(q1[cut:], v1)])
    p3, p2, q1, s0, t0, s1 = joined(p3, p2, q1, s0, t0, s1)
    i1, i2, y1, p0, q0, p1 = joined(
        send(p3, middle), send(p2, inward), cross(q1, 1), *experts(s0, t0, s1)
    )
    p1, p2 = plus(p1, y1, i1), plus(p2, i2)
    return plus(p0, cross(q0, 1), cross(p1, 2), send(p2, middle))


def direct_plan(mine, nodes, cross, experts):
    blocks = {0: mine}
    for step in range(2, nodes, 2):
        blocks[step] = cross(mine, step)
    for step in range(0, nodes, 2):
        blocks[step + 1] = cross(blocks[step], 1)
    shares = {}
    group = min(nodes, 4)
    for first in range(0, nodes, group):
        steps = range(first, first + group)
        shares.update(zip(steps, experts(*[blocks[s] for s in steps])))
    sums = []
    for step in range(0, nodes, 2):
        part = plus(shares[step], cross(shares[step + 1], 1))
        sums.append(cross(part, step) if step else part)
    return plus(*sums)


def solution(mesh):
    return jax.shard_map(
        per_device,
        mesh=mesh,
        in_specs=(
            P(("rep", "node", "local"), None),
            P(("rep", "node", "local"), None),
            P(("rep", "node", "local"), None),
            P("node", None, "local"),
            P("node", None, "local"),
            P("node", "local", None),
        ),
        out_specs=P(("rep", "node", "local"), None),
        check_vma=False,
    )
```

```python
import functools

import jax
import jax.numpy as jnp
from jax import lax
from jax.experimental import pallas as pl
from jax.experimental.pallas import tpu as pltpu
from jax.sharding import PartitionSpec as P

LANES = 128
RING = 3
KERNEL_VMEM = 50 * 1024 * 1024


def divisor_tile(extent, most, unit):
    best = unit
    for tile in range(unit, most + 1, unit):
        if extent % tile == 0:
            best = tile
    return best


def expert_kernel(count, slab, out_tile, *refs):
    blocks = refs[:count]
    node, gate_own, up_own, gate_other, up_other, down_own, down_other = refs[count : count + 7]
    results = refs[count + 7 : 2 * count + 7]
    rows, gates, ups, downs, gate_sum, up_sum, hidden, staged = refs[2 * count + 7 : 2 * count + 15]
    block_sem, gate_sem, up_sem, down_sem, out_sem = refs[2 * count + 15 :]
    heights = [block.shape[0] for block in blocks]
    starts = [sum(heights[:i]) for i in range(count)]
    _, width, depth = gate_own.shape
    slabs = width // slab
    tiles = width // out_tile

    def block_copy(i):
        return pltpu.make_async_copy(
            blocks[i], rows.at[pl.ds(starts[i], heights[i])], block_sem.at[i]
        )

    def slab_copies(gate, up, index, slot):
        place = pl.ds(pl.multiple_of(index * slab, slab), slab)
        return (
            pltpu.make_async_copy(gate.at[0, place], gates.at[slot], gate_sem.at[slot]),
            pltpu.make_async_copy(up.at[0, place], ups.at[slot], up_sem.at[slot]),
        )

    def down_copies(tile):
        slot = lax.rem(tile, RING)
        place = pl.ds(pl.multiple_of(tile * out_tile, out_tile), out_tile)
        return (
            pltpu.make_async_copy(down_own.at[0, :, place], downs.at[slot, 0], down_sem.at[slot, 0]),
            pltpu.make_async_copy(down_other.at[0, :, place], downs.at[slot, 1], down_sem.at[slot, 1]),
        )

    def start_load(index):
        slot = lax.rem(index, RING)

        @pl.when(index < slabs)
        def own():
            for copy in slab_copies(gate_own, up_own, index, slot):
                copy.start()

        @pl.when((index >= slabs) & (index < 2 * slabs))
        def other():
            for copy in slab_copies(gate_other, up_other, index - slabs, slot):
                copy.start()

        @pl.when((index >= 2 * slabs) & (index < 2 * slabs + tiles))
        def down():
            for copy in down_copies(index - 2 * slabs):
                copy.start()

    def out_copies(tile, slot):
        place = pl.ds(pl.multiple_of(tile * out_tile, out_tile), out_tile)
        return [
            pltpu.make_async_copy(
                staged.at[slot, pl.ds(starts[i], heights[i])],
                results[i].at[:, place],
                out_sem.at[slot, i],
            )
            for i in range(count)
        ]

    for i in range(count):
        block_copy(i).start()
    for index in range(RING):
        start_load(jnp.int32(index))
    for i in range(count):
        block_copy(i).wait()

    def project(index, half):
        slot = lax.rem(index, RING)
        local = index - half * slabs
        for copy in slab_copies(gate_own, up_own, local, slot):
            copy.wait()
        piece = rows[:, pl.ds(pl.multiple_of(local * slab, slab), slab)]
        gate_part = jnp.dot(piece, gates[slot], preferred_element_type=jnp.float32)
        up_part = jnp.dot(piece, ups[slot], preferred_element_type=jnp.float32)

        @pl.when(local == 0)
        def first():
            gate_sum[...] = gate_part
            up_sum[...] = up_part

        @pl.when(local > 0)
        def later():
            gate_sum[...] += gate_part
            up_sum[...] += up_part

        start_load(index + RING)

    for half in range(2):
        lax.fori_loop(
            half * slabs, (half + 1) * slabs, lambda i, _, half=half: project(i, half), None
        )
        act = gate_sum[...]
        hidden[half] = (act / (1.0 + jnp.exp(-act)) * up_sum[...]).astype(jnp.bfloat16)

    table = rows[:, width:].astype(jnp.float32)
    lane = lax.broadcasted_iota(jnp.int32, table.shape, 1)
    scale = jnp.sum(jnp.where(lane == node[0], table, 0.0), axis=1, keepdims=True)

    def down(tile, _):
        slot = lax.rem(tile, RING)
        out_slot = lax.rem(tile, 2)
        for copy in down_copies(tile):
            copy.wait()
        total = jnp.dot(hidden[0], downs[slot, 0], preferred_element_type=jnp.float32)
        total += jnp.dot(hidden[1], downs[slot, 1], preferred_element_type=jnp.float32)
        start_load(2 * slabs + tile + RING)

        @pl.when(tile >= 2)
        def free():
            for copy in out_copies(tile - 2, out_slot):
                copy.wait()

        staged[out_slot] = (total * scale).astype(jnp.bfloat16)
        for copy in out_copies(tile, out_slot):
            copy.start()

    lax.fori_loop(0, tiles, down, None)
    for tile in range(max(0, tiles - 2), tiles):
        for copy in out_copies(tile, tile % 2):
            copy.wait()


def expert_rows(blocks, node, weights):
    count = len(blocks)
    total_width = blocks[0].shape[1]
    _, width, depth = weights[0].shape
    slab = divisor_tile(width, 1792, 128)
    out_tile = divisor_tile(width, 1024, 128)
    tiles = width // out_tile
    row_count = sum(block.shape[0] for block in blocks)
    anywhere = pl.BlockSpec(memory_space=pl.ANY)
    return pl.pallas_call(
        functools.partial(expert_kernel, count, slab, out_tile),
        in_specs=[anywhere] * count
        + [pl.BlockSpec(memory_space=pltpu.SMEM)]
        + [pl.BlockSpec(memory_space=pltpu.HBM)] * 6,
        out_specs=[anywhere] * count,
        out_shape=[jax.ShapeDtypeStruct((block.shape[0], width), jnp.bfloat16) for block in blocks],
        scratch_shapes=[
            pltpu.VMEM((row_count, total_width), jnp.bfloat16),
            pltpu.VMEM((RING, slab, depth), jnp.bfloat16),
            pltpu.VMEM((RING, slab, depth), jnp.bfloat16),
            pltpu.VMEM((RING, 2, depth, out_tile), jnp.bfloat16),
            pltpu.VMEM((row_count, depth), jnp.float32),
            pltpu.VMEM((row_count, depth), jnp.float32),
            pltpu.VMEM((2, row_count, depth), jnp.bfloat16),
            pltpu.VMEM((2, row_count, out_tile), jnp.bfloat16),
            pltpu.SemaphoreType.DMA((count,)),
            pltpu.SemaphoreType.DMA((RING,)),
            pltpu.SemaphoreType.DMA((RING,)),
            pltpu.SemaphoreType.DMA((RING, 2)),
            pltpu.SemaphoreType.DMA((2, count)),
        ],
        compiler_params=pltpu.CompilerParams(vmem_limit_bytes=KERNEL_VMEM),
        cost_estimate=pl.CostEstimate(
            flops=12 * row_count * width * depth,
            bytes_accessed=2 * (6 * width * depth + 2 * row_count * width),
            transcendentals=2 * row_count * depth,
        ),
    )(*blocks, node, *weights)


def joined(*arrays):
    return lax.optimization_barrier(arrays)


def plus(*arrays):
    total = arrays[0].astype(jnp.float32)
    for array in arrays[1:]:
        total = total + array.astype(jnp.float32)
    return total.astype(jnp.bfloat16)


def per_device(tokens, gate_ids, gate_values, w_gate, w_up, w_down):
    nodes = lax.axis_size("node")
    node = lax.axis_index("node")

    def send(array, pairs):
        return lax.ppermute(array, "node", pairs)

    def cross(array, step):
        return send(array, [(n, n ^ step) for n in range(nodes)])

    def swap(array):
        return lax.ppermute(array, "local", [(0, 1), (1, 0)])

    lanes = jnp.arange(LANES, dtype=jnp.int32)
    chosen = gate_ids[:, :, None] == lanes[None, None, :]
    table = jnp.sum(
        jnp.where(chosen, gate_values.astype(jnp.float32)[:, :, None], 0.0), axis=1
    ).astype(jnp.bfloat16)
    mine = jnp.concatenate([tokens, table], axis=1)

    place = node.astype(jnp.int32).reshape(1)

    def experts(others, *blocks):
        weights = [w_gate, w_up, others[0], others[1], w_down, others[2]]
        return expert_rows(blocks, place, weights)

    halves = (w_gate, w_up, w_down)
    if nodes == 8:
        return line_plan(mine, node, send, cross, swap, halves, experts)
    others = [swap(half) for half in halves]
    return direct_plan(mine, nodes, cross, functools.partial(experts, others))


def line_plan(mine, node, send, cross, swap, halves, experts):
    middle = [(2, 4), (4, 2), (3, 5), (5, 3)]
    outward = [(2, 0), (3, 1), (4, 6), (5, 7)]
    inward = [(b, a) for a, b in outward]
    inner = (node >= 2) & (node < 6)

    s0, (w_gate, w_up, w_down) = mine, halves
    cut = mine.shape[0] // 2
    v_gate, v_up = swap(w_gate), swap(w_up)
    s1, m2, t0, w_down = joined(cross(s0, 2), send(s0, middle), cross(s0, 1), w_down)
    v_gate, w_down = joined(v_gate, w_down)
    m3 = send(s1, middle)
    e2, t1, v_up, v_down = joined(send(m2, outward), cross(s1, 1), v_up, swap(w_down))
    experts = functools.partial(experts, (v_gate, v_up, v_down))
    s2 = jnp.where(inner, m2, e2)
    e3, t2, n3, q1, p2 = joined(
        send(m3, outward), cross(s2, 1), send(t1[cut:], middle), *experts(t1, s2)
    )
    t3, o3, s3 = joined(
        cross(jnp.where(inner, m3[:cut], e3[:cut]), 1), send(n3, outward), jnp.where(inner, m3, e3)
    )
    q2, p3, q3, r3, s0, t0, s1 = joined(
        *experts(t2, s3, t3, jnp.where(inner, n3, o3)), s0, t0, s1
    )

    y3, v3 = joined(cross(q3, 1), send(r3, inward))
    p3, r3 = jnp.concatenate([plus(p3[:cut], y3), p3[cut:]]), plus(r3, v3)
    i3, y2, v1 = joined(send(p3, inward), cross(q2, 1), send(r3, middle))
    p3, p2, q1 = plus(p3, i3), plus(p2, y2), jnp.concatenate([q1[:cut], plus(q1[cut:], v1)])
    p3, p2, q1, s0, t0, s1 = joined(p3, p2, q1, s0, t0, s1)
    i1, i2, y1, p0, q0, p1 = joined(
        send(p3, middle), send(p2, inward), cross(q1, 1), *experts(s0, t0, s1)
    )
    p1, p2 = plus(p1, y1, i1), plus(p2, i2)
    return plus(p0, cross(q0, 1), cross(p1, 2), send(p2, middle))


def direct_plan(mine, nodes, cross, experts):
    blocks = {0: mine}
    for step in range(2, nodes, 2):
        blocks[step] = cross(mine, step)
    for step in range(0, nodes, 2):
        blocks[step + 1] = cross(blocks[step], 1)
    shares = {}
    group = min(nodes, 4)
    for first in range(0, nodes, group):
        steps = range(first, first + group)
        shares.update(zip(steps, experts(*[blocks[s] for s in steps])))
    sums = []
    for step in range(0, nodes, 2):
        part = plus(shares[step], cross(shares[step + 1], 1))
        sums.append(cross(part, step) if step else part)
    return plus(*sums)


def solution(mesh):
    return jax.shard_map(
        per_device,
        mesh=mesh,
        in_specs=(
            P(("rep", "node", "local"), None),
            P(("rep", "node", "local"), None),
            P(("rep", "node", "local"), None),
            P("node", None, "local"),
            P("node", None, "local"),
            P("node", "local", None),
        ),
        out_specs=P(("rep", "node", "local"), None),
        check_vma=False,
    )
```

```python
import functools

import jax
import jax.numpy as jnp
from jax import lax
from jax.experimental import pallas as pl
from jax.experimental.pallas import tpu as pltpu
from jax.sharding import PartitionSpec as P

LANES = 128
RING = 3
KERNEL_VMEM = 50 * 1024 * 1024


def divisor_tile(extent, most, unit):
    best = unit
    for tile in range(unit, most + 1, unit):
        if extent % tile == 0:
            best = tile
    return best


def expert_kernel(count, slab, out_tile, *refs):
    blocks = refs[:count]
    node, gate_own, up_own, gate_other, up_other, down_own, down_other = refs[count : count + 7]
    results = refs[count + 7 : 2 * count + 7]
    rows, gates, ups, downs, gate_sum, up_sum, hidden, staged = refs[2 * count + 7 : 2 * count + 15]
    block_sem, gate_sem, up_sem, down_sem, out_sem = refs[2 * count + 15 :]
    heights = [block.shape[0] for block in blocks]
    starts = [sum(heights[:i]) for i in range(count)]
    _, width, depth = gate_own.shape
    slabs = width // slab
    tiles = width // out_tile

    def block_copy(i):
        return pltpu.make_async_copy(
            blocks[i], rows.at[pl.ds(starts[i], heights[i])], block_sem.at[i]
        )

    def slab_copies(gate, up, index, slot):
        place = pl.ds(pl.multiple_of(index * slab, slab), slab)
        return (
            pltpu.make_async_copy(gate.at[0, place], gates.at[slot], gate_sem.at[slot]),
            pltpu.make_async_copy(up.at[0, place], ups.at[slot], up_sem.at[slot]),
        )

    def down_copies(tile):
        slot = lax.rem(tile, RING)
        place = pl.ds(pl.multiple_of(tile * out_tile, out_tile), out_tile)
        return (
            pltpu.make_async_copy(down_own.at[0, :, place], downs.at[slot, 0], down_sem.at[slot, 0]),
            pltpu.make_async_copy(down_other.at[0, :, place], downs.at[slot, 1], down_sem.at[slot, 1]),
        )

    def start_load(index):
        slot = lax.rem(index, RING)

        @pl.when(index < slabs)
        def own():
            for copy in slab_copies(gate_own, up_own, index, slot):
                copy.start()

        @pl.when((index >= slabs) & (index < 2 * slabs))
        def other():
            for copy in slab_copies(gate_other, up_other, index - slabs, slot):
                copy.start()

        @pl.when((index >= 2 * slabs) & (index < 2 * slabs + tiles))
        def down():
            for copy in down_copies(index - 2 * slabs):
                copy.start()

    def out_copies(tile, slot):
        place = pl.ds(pl.multiple_of(tile * out_tile, out_tile), out_tile)
        return [
            pltpu.make_async_copy(
                staged.at[slot, pl.ds(starts[i], heights[i])],
                results[i].at[:, place],
                out_sem.at[slot, i],
            )
            for i in range(count)
        ]

    start_load(jnp.int32(0))
    for i in range(count):
        block_copy(i).start()
    for index in range(1, RING):
        start_load(jnp.int32(index))
    for i in range(count):
        block_copy(i).wait()

    def project(index, half):
        slot = lax.rem(index, RING)
        local = index - half * slabs
        for copy in slab_copies(gate_own, up_own, local, slot):
            copy.wait()
        piece = rows[:, pl.ds(pl.multiple_of(local * slab, slab), slab)]
        gate_part = jnp.dot(piece, gates[slot], preferred_element_type=jnp.float32)
        up_part = jnp.dot(piece, ups[slot], preferred_element_type=jnp.float32)

        @pl.when(local == 0)
        def first():
            gate_sum[...] = gate_part
            up_sum[...] = up_part

        @pl.when(local > 0)
        def later():
            gate_sum[...] += gate_part
            up_sum[...] += up_part

        start_load(index + RING)

    for half in range(2):
        lax.fori_loop(
            half * slabs, (half + 1) * slabs, lambda i, _, half=half: project(i, half), None
        )
        act = gate_sum[...]
        hidden[half] = (act / (1.0 + jnp.exp(-act)) * up_sum[...]).astype(jnp.bfloat16)

    table = rows[:, width:].astype(jnp.float32)
    lane = lax.broadcasted_iota(jnp.int32, table.shape, 1)
    scale = jnp.sum(jnp.where(lane == node[0], table, 0.0), axis=1, keepdims=True)

    def down(tile, _):
        slot = lax.rem(tile, RING)
        out_slot = lax.rem(tile, 2)
        for copy in down_copies(tile):
            copy.wait()
        total = jnp.dot(hidden[0], downs[slot, 0], preferred_element_type=jnp.float32)
        total += jnp.dot(hidden[1], downs[slot, 1], preferred_element_type=jnp.float32)
        start_load(2 * slabs + tile + RING)

        @pl.when(tile >= 2)
        def free():
            for copy in out_copies(tile - 2, out_slot):
                copy.wait()

        staged[out_slot] = (total * scale).astype(jnp.bfloat16)
        for copy in out_copies(tile, out_slot):
            copy.start()

    lax.fori_loop(0, tiles, down, None)
    for tile in range(max(0, tiles - 2), tiles):
        for copy in out_copies(tile, tile % 2):
            copy.wait()


def expert_rows(blocks, node, weights):
    count = len(blocks)
    total_width = blocks[0].shape[1]
    _, width, depth = weights[0].shape
    slab = divisor_tile(width, 1792, 128)
    out_tile = divisor_tile(width, 1792, 128)
    tiles = width // out_tile
    row_count = sum(block.shape[0] for block in blocks)
    anywhere = pl.BlockSpec(memory_space=pl.ANY)
    return pl.pallas_call(
        functools.partial(expert_kernel, count, slab, out_tile),
        in_specs=[anywhere] * count
        + [pl.BlockSpec(memory_space=pltpu.SMEM)]
        + [pl.BlockSpec(memory_space=pltpu.HBM)] * 6,
        out_specs=[anywhere] * count,
        out_shape=[jax.ShapeDtypeStruct((block.shape[0], width), jnp.bfloat16) for block in blocks],
        scratch_shapes=[
            pltpu.VMEM((row_count, total_width), jnp.bfloat16),
            pltpu.VMEM((RING, slab, depth), jnp.bfloat16),
            pltpu.VMEM((RING, slab, depth), jnp.bfloat16),
            pltpu.VMEM((RING, 2, depth, out_tile), jnp.bfloat16),
            pltpu.VMEM((row_count, depth), jnp.float32),
            pltpu.VMEM((row_count, depth), jnp.float32),
            pltpu.VMEM((2, row_count, depth), jnp.bfloat16),
            pltpu.VMEM((2, row_count, out_tile), jnp.bfloat16),
            pltpu.SemaphoreType.DMA((count,)),
            pltpu.SemaphoreType.DMA((RING,)),
            pltpu.SemaphoreType.DMA((RING,)),
            pltpu.SemaphoreType.DMA((RING, 2)),
            pltpu.SemaphoreType.DMA((2, count)),
        ],
        compiler_params=pltpu.CompilerParams(vmem_limit_bytes=KERNEL_VMEM),
        cost_estimate=pl.CostEstimate(
            flops=12 * row_count * width * depth,
            bytes_accessed=2 * (6 * width * depth + 2 * row_count * width),
            transcendentals=2 * row_count * depth,
        ),
    )(*blocks, node, *weights)


def joined(*arrays):
    return lax.optimization_barrier(arrays)


def plus(*arrays):
    total = arrays[0].astype(jnp.float32)
    for array in arrays[1:]:
        total = total + array.astype(jnp.float32)
    return total.astype(jnp.bfloat16)


def per_device(tokens, gate_ids, gate_values, w_gate, w_up, w_down):
    nodes = lax.axis_size("node")
    node = lax.axis_index("node")

    def send(array, pairs):
        return lax.ppermute(array, "node", pairs)

    def cross(array, step):
        return send(array, [(n, n ^ step) for n in range(nodes)])

    def swap(array):
        return lax.ppermute(array, "local", [(0, 1), (1, 0)])

    lanes = jnp.arange(LANES, dtype=jnp.int32)
    chosen = gate_ids[:, :, None] == lanes[None, None, :]
    table = jnp.sum(
        jnp.where(chosen, gate_values.astype(jnp.float32)[:, :, None], 0.0), axis=1
    ).astype(jnp.bfloat16)
    mine = jnp.concatenate([tokens, table], axis=1)

    place = node.astype(jnp.int32).reshape(1)

    def experts(others, *blocks):
        weights = [w_gate, w_up, others[0], others[1], w_down, others[2]]
        return expert_rows(blocks, place, weights)

    halves = (w_gate, w_up, w_down)
    if nodes == 8:
        return line_plan(mine, node, send, cross, swap, halves, experts)
    others = [swap(half) for half in halves]
    return direct_plan(mine, nodes, cross, functools.partial(experts, others))


def line_plan(mine, node, send, cross, swap, halves, experts):
    middle = [(2, 4), (4, 2), (3, 5), (5, 3)]
    outward = [(2, 0), (3, 1), (4, 6), (5, 7)]
    inward = [(b, a) for a, b in outward]
    inner = (node >= 2) & (node < 6)

    s0, (w_gate, w_up, w_down) = mine, halves
    cut = mine.shape[0] // 2
    v_gate, v_up = swap(w_gate), swap(w_up)
    s1, m2, t0, w_down = joined(cross(s0, 2), send(s0, middle), cross(s0, 1), w_down)
    v_gate, w_down = joined(v_gate, w_down)
    m3 = send(s1, middle)
    e2, t1, v_up, v_down = joined(send(m2, outward), cross(s1, 1), v_up, swap(w_down))
    experts = functools.partial(experts, (v_gate, v_up, v_down))
    s2 = jnp.where(inner, m2, e2)
    e3, t2, n3, q1, p2 = joined(
        send(m3, outward), cross(s2, 1), send(t1[cut:], middle), *experts(t1, s2)
    )
    t3, o3, s3 = joined(
        cross(jnp.where(inner, m3[:cut], e3[:cut]), 1), send(n3, outward), jnp.where(inner, m3, e3)
    )
    q2, p3, q3, r3, s0, t0, s1 = joined(
        *experts(t2, s3, t3, jnp.where(inner, n3, o3)), s0, t0, s1
    )

    y3, v3 = joined(cross(q3, 1), send(r3, inward))
    p3, r3 = jnp.concatenate([plus(p3[:cut], y3), p3[cut:]]), plus(r3, v3)
    i3, y2, v1 = joined(send(p3, inward), cross(q2, 1), send(r3, middle))
    p3, p2, q1 = plus(p3, i3), plus(p2, y2), jnp.concatenate([q1[:cut], plus(q1[cut:], v1)])
    p3, p2, q1, s0, t0, s1 = joined(p3, p2, q1, s0, t0, s1)
    i1, i2, y1, p0, q0, p1 = joined(
        send(p3, middle), send(p2, inward), cross(q1, 1), *experts(s0, t0, s1)
    )
    p1, p2 = plus(p1, y1, i1), plus(p2, i2)
    return plus(p0, cross(q0, 1), cross(p1, 2), send(p2, middle))


def direct_plan(mine, nodes, cross, experts):
    blocks = {0: mine}
    for step in range(2, nodes, 2):
        blocks[step] = cross(mine, step)
    for step in range(0, nodes, 2):
        blocks[step + 1] = cross(blocks[step], 1)
    shares = {}
    group = min(nodes, 4)
    for first in range(0, nodes, group):
        steps = range(first, first + group)
        shares.update(zip(steps, experts(*[blocks[s] for s in steps])))
    sums = []
    for step in range(0, nodes, 2):
        part = plus(shares[step], cross(shares[step + 1], 1))
        sums.append(cross(part, step) if step else part)
    return plus(*sums)


def solution(mesh):
    return jax.shard_map(
        per_device,
        mesh=mesh,
        in_specs=(
            P(("rep", "node", "local"), None),
            P(("rep", "node", "local"), None),
            P(("rep", "node", "local"), None),
            P("node", None, "local"),
            P("node", None, "local"),
            P("node", "local", None),
        ),
        out_specs=P(("rep", "node", "local"), None),
        check_vma=False,
    )
```

```python
import functools

import jax
import jax.numpy as jnp
from jax import lax
from jax.experimental import pallas as pl
from jax.experimental.pallas import tpu as pltpu
from jax.sharding import PartitionSpec as P

LANES = 128
RING = 4
KERNEL_VMEM = 50 * 1024 * 1024


def divisor_tile(extent, most, unit):
    best = unit
    for tile in range(unit, most + 1, unit):
        if extent % tile == 0:
            best = tile
    return best


def expert_kernel(count, slab, out_tile, *refs):
    blocks = refs[:count]
    node, gate_own, up_own, gate_other, up_other, down_own, down_other = refs[count : count + 7]
    results = refs[count + 7 : 2 * count + 7]
    rows, gates, ups, downs, gate_sum, up_sum, hidden, staged = refs[2 * count + 7 : 2 * count + 15]
    block_sem, gate_sem, up_sem, down_sem, out_sem = refs[2 * count + 15 :]
    heights = [block.shape[0] for block in blocks]
    starts = [sum(heights[:i]) for i in range(count)]
    _, width, depth = gate_own.shape
    slabs = width // slab
    tiles = width // out_tile

    def block_copy(i):
        return pltpu.make_async_copy(
            blocks[i], rows.at[pl.ds(starts[i], heights[i])], block_sem.at[i]
        )

    def slab_copies(gate, up, index, slot):
        place = pl.ds(pl.multiple_of(index * slab, slab), slab)
        return (
            pltpu.make_async_copy(gate.at[0, place], gates.at[slot], gate_sem.at[slot]),
            pltpu.make_async_copy(up.at[0, place], ups.at[slot], up_sem.at[slot]),
        )

    def down_copies(tile):
        slot = lax.rem(tile, RING)
        place = pl.ds(pl.multiple_of(tile * out_tile, out_tile), out_tile)
        return (
            pltpu.make_async_copy(down_own.at[0, :, place], downs.at[slot, 0], down_sem.at[slot, 0]),
            pltpu.make_async_copy(down_other.at[0, :, place], downs.at[slot, 1], down_sem.at[slot, 1]),
        )

    def start_load(index):
        slot = lax.rem(index, RING)

        @pl.when(index < slabs)
        def own():
            for copy in slab_copies(gate_own, up_own, index, slot):
                copy.start()

        @pl.when((index >= slabs) & (index < 2 * slabs))
        def other():
            for copy in slab_copies(gate_other, up_other, index - slabs, slot):
                copy.start()

        @pl.when((index >= 2 * slabs) & (index < 2 * slabs + tiles))
        def down():
            for copy in down_copies(index - 2 * slabs):
                copy.start()

    def out_copies(tile, slot):
        place = pl.ds(pl.multiple_of(tile * out_tile, out_tile), out_tile)
        return [
            pltpu.make_async_copy(
                staged.at[slot, pl.ds(starts[i], heights[i])],
                results[i].at[:, place],
                out_sem.at[slot, i],
            )
            for i in range(count)
        ]

    start_load(jnp.int32(0))
    for i in range(count):
        block_copy(i).start()
    for index in range(1, RING):
        start_load(jnp.int32(index))
    for i in range(count):
        block_copy(i).wait()

    table = rows[:, width:].astype(jnp.float32)
    lane = lax.broadcasted_iota(jnp.int32, table.shape, 1)
    scale = jnp.sum(jnp.where(lane == node[0], table, 0.0), axis=1, keepdims=True)

    def project(index, half):
        slot = lax.rem(index, RING)
        local = index - half * slabs
        for copy in slab_copies(gate_own, up_own, local, slot):
            copy.wait()
        piece = rows[:, pl.ds(pl.multiple_of(local * slab, slab), slab)]
        gate_part = jnp.dot(piece, gates[slot], preferred_element_type=jnp.float32)
        up_part = jnp.dot(piece, ups[slot], preferred_element_type=jnp.float32)

        @pl.when(local == 0)
        def first():
            gate_sum[...] = gate_part
            up_sum[...] = up_part

        @pl.when(local > 0)
        def later():
            gate_sum[...] += gate_part
            up_sum[...] += up_part

        start_load(index + RING)

    for half in range(2):
        lax.fori_loop(
            half * slabs, (half + 1) * slabs, lambda i, _, half=half: project(i, half), None
        )
        act = gate_sum[...]
        hidden[half] = (act / (1.0 + jnp.exp(-act)) * up_sum[...]).astype(jnp.bfloat16)

    def down(tile, _):
        slot = lax.rem(tile, RING)
        out_slot = lax.rem(tile, 2)
        for copy in down_copies(tile):
            copy.wait()
        total = jnp.dot(hidden[0], downs[slot, 0], preferred_element_type=jnp.float32)
        total += jnp.dot(hidden[1], downs[slot, 1], preferred_element_type=jnp.float32)
        start_load(2 * slabs + tile + RING)

        @pl.when(tile >= 2)
        def free():
            for copy in out_copies(tile - 2, out_slot):
                copy.wait()

        staged[out_slot] = (total * scale).astype(jnp.bfloat16)
        for copy in out_copies(tile, out_slot):
            copy.start()

    lax.fori_loop(0, tiles, down, None)
    for tile in range(max(0, tiles - 2), tiles):
        for copy in out_copies(tile, tile % 2):
            copy.wait()


def expert_rows(blocks, node, weights):
    count = len(blocks)
    total_width = blocks[0].shape[1]
    _, width, depth = weights[0].shape
    slab = divisor_tile(width, 1792, 128)
    out_tile = divisor_tile(width, 1792, 128)
    tiles = width // out_tile
    row_count = sum(block.shape[0] for block in blocks)
    anywhere = pl.BlockSpec(memory_space=pl.ANY)
    return pl.pallas_call(
        functools.partial(expert_kernel, count, slab, out_tile),
        in_specs=[anywhere] * count
        + [pl.BlockSpec(memory_space=pltpu.SMEM)]
        + [pl.BlockSpec(memory_space=pltpu.HBM)] * 6,
        out_specs=[anywhere] * count,
        out_shape=[jax.ShapeDtypeStruct((block.shape[0], width), jnp.bfloat16) for block in blocks],
        scratch_shapes=[
            pltpu.VMEM((row_count, total_width), jnp.bfloat16),
            pltpu.VMEM((RING, slab, depth), jnp.bfloat16),
            pltpu.VMEM((RING, slab, depth), jnp.bfloat16),
            pltpu.VMEM((RING, 2, depth, out_tile), jnp.bfloat16),
            pltpu.VMEM((row_count, depth), jnp.float32),
            pltpu.VMEM((row_count, depth), jnp.float32),
            pltpu.VMEM((2, row_count, depth), jnp.bfloat16),
            pltpu.VMEM((2, row_count, out_tile), jnp.bfloat16),
            pltpu.SemaphoreType.DMA((count,)),
            pltpu.SemaphoreType.DMA((RING,)),
            pltpu.SemaphoreType.DMA((RING,)),
            pltpu.SemaphoreType.DMA((RING, 2)),
            pltpu.SemaphoreType.DMA((2, count)),
        ],
        compiler_params=pltpu.CompilerParams(vmem_limit_bytes=KERNEL_VMEM),
        cost_estimate=pl.CostEstimate(
            flops=12 * row_count * width * depth,
            bytes_accessed=2 * (6 * width * depth + 2 * row_count * width),
            transcendentals=2 * row_count * depth,
        ),
    )(*blocks, node, *weights)


def joined(*arrays):
    return lax.optimization_barrier(arrays)


def plus(*arrays):
    total = arrays[0].astype(jnp.float32)
    for array in arrays[1:]:
        total = total + array.astype(jnp.float32)
    return total.astype(jnp.bfloat16)


def per_device(tokens, gate_ids, gate_values, w_gate, w_up, w_down):
    nodes = lax.axis_size("node")
    node = lax.axis_index("node")

    def send(array, pairs):
        return lax.ppermute(array, "node", pairs)

    def cross(array, step):
        return send(array, [(n, n ^ step) for n in range(nodes)])

    def swap(array):
        return lax.ppermute(array, "local", [(0, 1), (1, 0)])

    lanes = jnp.arange(LANES, dtype=jnp.int32)
    chosen = gate_ids[:, :, None] == lanes[None, None, :]
    table = jnp.sum(
        jnp.where(chosen, gate_values.astype(jnp.float32)[:, :, None], 0.0), axis=1
    ).astype(jnp.bfloat16)
    mine = jnp.concatenate([tokens, table], axis=1)

    place = node.astype(jnp.int32).reshape(1)

    def experts(others, *blocks):
        weights = [w_gate, w_up, others[0], others[1], w_down, others[2]]
        return expert_rows(blocks, place, weights)

    halves = (w_gate, w_up, w_down)
    if nodes == 8:
        return line_plan(mine, node, send, cross, swap, halves, experts)
    others = [swap(half) for half in halves]
    return direct_plan(mine, nodes, cross, functools.partial(experts, others))


def line_plan(mine, node, send, cross, swap, halves, experts):
    middle = [(2, 4), (4, 2), (3, 5), (5, 3)]
    outward = [(2, 0), (3, 1), (4, 6), (5, 7)]
    inward = [(b, a) for a, b in outward]
    inner = (node >= 2) & (node < 6)

    s0, (w_gate, w_up, w_down) = mine, halves
    cut = mine.shape[0] // 2
    v_gate, v_up = swap(w_gate), swap(w_up)
    s1, m2, t0, w_down = joined(cross(s0, 2), send(s0, middle), cross(s0, 1), w_down)
    v_gate, w_down = joined(v_gate, w_down)
    m3 = send(s1, middle)
    e2, t1, v_up, v_down = joined(send(m2, outward), cross(s1, 1), v_up, swap(w_down))
    experts = functools.partial(experts, (v_gate, v_up, v_down))
    s2 = jnp.where(inner, m2, e2)
    e3, t2, n3, q1, p2 = joined(
        send(m3, outward), cross(s2, 1), send(t1[cut:], middle), *experts(t1, s2)
    )
    t3, o3, s3 = joined(
        cross(jnp.where(inner, m3[:cut], e3[:cut]), 1), send(n3, outward), jnp.where(inner, m3, e3)
    )
    q2, p3, q3, r3, s0, t0, s1 = joined(
        *experts(t2, s3, t3, jnp.where(inner, n3, o3)), s0, t0, s1
    )

    y3, v3 = joined(cross(q3, 1), send(r3, inward))
    p3, r3 = jnp.concatenate([plus(p3[:cut], y3), p3[cut:]]), plus(r3, v3)
    i3, y2, v1 = joined(send(p3, inward), cross(q2, 1), send(r3, middle))
    p3, p2, q1 = plus(p3, i3), plus(p2, y2), jnp.concatenate([q1[:cut], plus(q1[cut:], v1)])
    p3, p2, q1, s0, t0, s1 = joined(p3, p2, q1, s0, t0, s1)
    i1, i2, y1, p0, q0, p1 = joined(
        send(p3, middle), send(p2, inward), cross(q1, 1), *experts(s0, t0, s1)
    )
    p1, p2 = plus(p1, y1, i1), plus(p2, i2)
    return plus(p0, cross(q0, 1), cross(p1, 2), send(p2, middle))


def direct_plan(mine, nodes, cross, experts):
    blocks = {0: mine}
    for step in range(2, nodes, 2):
        blocks[step] = cross(mine, step)
    for step in range(0, nodes, 2):
        blocks[step + 1] = cross(blocks[step], 1)
    shares = {}
    group = min(nodes, 4)
    for first in range(0, nodes, group):
        steps = range(first, first + group)
        shares.update(zip(steps, experts(*[blocks[s] for s in steps])))
    sums = []
    for step in range(0, nodes, 2):
        part = plus(shares[step], cross(shares[step + 1], 1))
        sums.append(cross(part, step) if step else part)
    return plus(*sums)


def solution(mesh):
    return jax.shard_map(
        per_device,
        mesh=mesh,
        in_specs=(
            P(("rep", "node", "local"), None),
            P(("rep", "node", "local"), None),
            P(("rep", "node", "local"), None),
            P("node", None, "local"),
            P("node", None, "local"),
            P("node", "local", None),
        ),
        out_specs=P(("rep", "node", "local"), None),
        check_vma=False,
    )
```

```python
import functools

import jax
import jax.numpy as jnp
from jax import lax
from jax.experimental import pallas as pl
from jax.experimental.pallas import tpu as pltpu
from jax.sharding import PartitionSpec as P

LANES = 128
RING = 3
KERNEL_VMEM = 50 * 1024 * 1024


def divisor_tile(extent, most, unit):
    best = unit
    for tile in range(unit, most + 1, unit):
        if extent % tile == 0:
            best = tile
    return best


def expert_kernel(count, slab, out_tile, *refs):
    blocks = refs[:count]
    node, gate_own, up_own, gate_other, up_other, down_own, down_other = refs[count : count + 7]
    results = refs[count + 7 : 2 * count + 7]
    rows, gates, ups, downs, gate_sum, up_sum, hidden, staged = refs[2 * count + 7 : 2 * count + 15]
    block_sem, gate_sem, up_sem, down_sem, out_sem = refs[2 * count + 15 :]
    heights = [block.shape[0] for block in blocks]
    starts = [sum(heights[:i]) for i in range(count)]
    _, width, depth = gate_own.shape
    slabs = width // slab
    tiles = width // out_tile

    def block_copy(i):
        return pltpu.make_async_copy(
            blocks[i], rows.at[pl.ds(starts[i], heights[i])], block_sem.at[i]
        )

    def slab_copies(gate, up, index, slot):
        place = pl.ds(pl.multiple_of(index * slab, slab), slab)
        return (
            pltpu.make_async_copy(gate.at[0, place], gates.at[slot], gate_sem.at[slot]),
            pltpu.make_async_copy(up.at[0, place], ups.at[slot], up_sem.at[slot]),
        )

    def down_copies(tile):
        slot = lax.rem(tile, RING)
        place = pl.ds(pl.multiple_of(tile * out_tile, out_tile), out_tile)
        return (
            pltpu.make_async_copy(down_own.at[0, :, place], downs.at[slot, 0], down_sem.at[slot, 0]),
            pltpu.make_async_copy(down_other.at[0, :, place], downs.at[slot, 1], down_sem.at[slot, 1]),
        )

    def start_load(index):
        slot = lax.rem(index, RING)

        @pl.when(index < slabs)
        def own():
            for copy in slab_copies(gate_own, up_own, index, slot):
                copy.start()

        @pl.when((index >= slabs) & (index < 2 * slabs))
        def other():
            for copy in slab_copies(gate_other, up_other, index - slabs, slot):
                copy.start()

        @pl.when((index >= 2 * slabs) & (index < 2 * slabs + tiles))
        def down():
            for copy in down_copies(index - 2 * slabs):
                copy.start()

    def out_copies(tile, slot):
        place = pl.ds(pl.multiple_of(tile * out_tile, out_tile), out_tile)
        return [
            pltpu.make_async_copy(
                staged.at[slot, pl.ds(starts[i], heights[i])],
                results[i].at[:, place],
                out_sem.at[slot, i],
            )
            for i in range(count)
        ]

    start_load(jnp.int32(0))
    for i in range(count):
        block_copy(i).start()
    for index in range(1, RING):
        start_load(jnp.int32(index))
    for i in range(count):
        block_copy(i).wait()

    def project(index, half):
        slot = lax.rem(index, RING)
        local = index - half * slabs
        for copy in slab_copies(gate_own, up_own, local, slot):
            copy.wait()
        piece = rows[:, pl.ds(pl.multiple_of(local * slab, slab), slab)]
        gate_part = jnp.dot(piece, gates[slot], preferred_element_type=jnp.float32)
        up_part = jnp.dot(piece, ups[slot], preferred_element_type=jnp.float32)

        @pl.when(local == 0)
        def first():
            gate_sum[...] = gate_part
            up_sum[...] = up_part

        @pl.when(local > 0)
        def later():
            gate_sum[...] += gate_part
            up_sum[...] += up_part

        start_load(index + RING)

    for half in range(2):
        lax.fori_loop(
            half * slabs, (half + 1) * slabs, lambda i, _, half=half: project(i, half), None
        )
        act = gate_sum[...]
        hidden[half] = (act / (1.0 + jnp.exp(-act)) * up_sum[...]).astype(jnp.bfloat16)

    table = rows[:, width:].astype(jnp.float32)
    lane = lax.broadcasted_iota(jnp.int32, table.shape, 1)
    scale = jnp.sum(jnp.where(lane == node[0], table, 0.0), axis=1, keepdims=True)

    def down(tile, _):
        slot = lax.rem(tile, RING)
        out_slot = lax.rem(tile, 2)
        for copy in down_copies(tile):
            copy.wait()
        total = jnp.dot(hidden[0], downs[slot, 0], preferred_element_type=jnp.float32)
        total += jnp.dot(hidden[1], downs[slot, 1], preferred_element_type=jnp.float32)
        start_load(2 * slabs + tile + RING)

        @pl.when(tile >= 2)
        def free():
            for copy in out_copies(tile - 2, out_slot):
                copy.wait()

        staged[out_slot] = (total * scale).astype(jnp.bfloat16)
        for copy in out_copies(tile, out_slot):
            copy.start()

    lax.fori_loop(0, tiles, down, None)
    for tile in range(max(0, tiles - 2), tiles):
        for copy in out_copies(tile, tile % 2):
            copy.wait()


def expert_rows(blocks, node, weights):
    count = len(blocks)
    total_width = blocks[0].shape[1]
    _, width, depth = weights[0].shape
    slab = divisor_tile(width, 1792, 128)
    out_tile = divisor_tile(width, 1792, 128)
    tiles = width // out_tile
    row_count = sum(block.shape[0] for block in blocks)
    anywhere = pl.BlockSpec(memory_space=pl.ANY)
    return pl.pallas_call(
        functools.partial(expert_kernel, count, slab, out_tile),
        in_specs=[anywhere] * count
        + [pl.BlockSpec(memory_space=pltpu.SMEM)]
        + [pl.BlockSpec(memory_space=pltpu.HBM)] * 6,
        out_specs=[anywhere] * count,
        out_shape=[jax.ShapeDtypeStruct((block.shape[0], width), jnp.bfloat16) for block in blocks],
        scratch_shapes=[
            pltpu.VMEM((row_count, total_width), jnp.bfloat16),
            pltpu.VMEM((RING, slab, depth), jnp.bfloat16),
            pltpu.VMEM((RING, slab, depth), jnp.bfloat16),
            pltpu.VMEM((RING, 2, depth, out_tile), jnp.bfloat16),
            pltpu.VMEM((row_count, depth), jnp.float32),
            pltpu.VMEM((row_count, depth), jnp.float32),
            pltpu.VMEM((2, row_count, depth), jnp.bfloat16),
            pltpu.VMEM((2, row_count, out_tile), jnp.bfloat16),
            pltpu.SemaphoreType.DMA((count,)),
            pltpu.SemaphoreType.DMA((RING,)),
            pltpu.SemaphoreType.DMA((RING,)),
            pltpu.SemaphoreType.DMA((RING, 2)),
            pltpu.SemaphoreType.DMA((2, count)),
        ],
        compiler_params=pltpu.CompilerParams(vmem_limit_bytes=KERNEL_VMEM),
        cost_estimate=pl.CostEstimate(
            flops=12 * row_count * width * depth,
            bytes_accessed=2 * (6 * width * depth + 2 * row_count * width),
            transcendentals=2 * row_count * depth,
        ),
    )(*blocks, node, *weights)


def joined(*arrays):
    return lax.optimization_barrier(arrays)


def plus(*arrays):
    total = arrays[0].astype(jnp.float32)
    for array in arrays[1:]:
        total = total + array.astype(jnp.float32)
    return total.astype(jnp.bfloat16)


def per_device(tokens, gate_ids, gate_values, w_gate, w_up, w_down):
    nodes = lax.axis_size("node")
    node = lax.axis_index("node")

    def send(array, pairs):
        return lax.ppermute(array, "node", pairs)

    def cross(array, step):
        return send(array, [(n, n ^ step) for n in range(nodes)])

    def swap(array):
        return lax.ppermute(array, "local", [(0, 1), (1, 0)])

    lanes = jnp.arange(LANES, dtype=jnp.int32)
    chosen = gate_ids[:, :, None] == lanes[None, None, :]
    table = jnp.sum(
        jnp.where(chosen, gate_values.astype(jnp.float32)[:, :, None], 0.0), axis=1
    ).astype(jnp.bfloat16)
    mine = jnp.concatenate([tokens, table], axis=1)

    place = node.astype(jnp.int32).reshape(1)

    def experts(others, *blocks):
        weights = [w_gate, w_up, others[0], others[1], w_down, others[2]]
        return expert_rows(blocks, place, weights)

    halves = (w_gate, w_up, w_down)
    if nodes == 8:
        return line_plan(mine, node, send, cross, swap, halves, experts)
    others = [swap(half) for half in halves]
    return direct_plan(mine, nodes, cross, functools.partial(experts, others))


def line_plan(mine, node, send, cross, swap, halves, experts):
    middle = [(2, 4), (4, 2), (3, 5), (5, 3)]
    outward = [(2, 0), (3, 1), (4, 6), (5, 7)]
    inward = [(b, a) for a, b in outward]
    inner = (node >= 2) & (node < 6)

    s0, (w_gate, w_up, w_down) = mine, halves
    cut = mine.shape[0] // 2
    v_gate, v_up = swap(w_gate), swap(w_up)
    s1, m2, t0, w_down = joined(cross(s0, 2), send(s0, middle), cross(s0, 1), w_down)
    v_gate, w_down = joined(v_gate, w_down)
    m3 = send(s1, middle)
    e2, t1, v_up, v_down = joined(send(m2, outward), cross(s1, 1), v_up, swap(w_down))
    experts = functools.partial(experts, (v_gate, v_up, v_down))
    s2 = jnp.where(inner, m2, e2)
    e3, t2, n3, q1, p2 = joined(
        send(m3, outward), cross(s2, 1), send(t1[cut:], middle), *experts(t1, s2)
    )
    t3, o3, s3 = joined(
        cross(jnp.where(inner, m3[:cut], e3[:cut]), 1), send(n3, outward), jnp.where(inner, m3, e3)
    )
    q2, p3, q3, r3, s0, t0, s1 = joined(
        *experts(t2, s3, t3, jnp.where(inner, n3, o3)), s0, t0, s1
    )

    y3, v3 = joined(cross(q3, 1), send(r3, inward))
    p3, r3 = jnp.concatenate([plus(p3[:cut], y3), p3[cut:]]), plus(r3, v3)
    near = q1[:cut]
    i3, y2, v1 = joined(send(p3, inward), cross(q2, 1), send(r3, middle))
    p3, p2, q1 = plus(p3, i3), plus(p2, y2), plus(q1[cut:], v1)
    p3, p2, q1, s0, t0, s1 = joined(p3, p2, q1, s0, t0, s1)
    i1, i2, y1, z1, p0, q0, p1 = joined(
        send(p3, middle), send(p2, inward), cross(near, 1), cross(q1, 1), *experts(s0, t0, s1)
    )
    p1, p2 = plus(p1, jnp.concatenate([y1, z1]), i1), plus(p2, i2)
    return plus(p0, cross(q0, 1), cross(p1, 2), send(p2, middle))


def direct_plan(mine, nodes, cross, experts):
    blocks = {0: mine}
    for step in range(2, nodes, 2):
        blocks[step] = cross(mine, step)
    for step in range(0, nodes, 2):
        blocks[step + 1] = cross(blocks[step], 1)
    shares = {}
    group = min(nodes, 4)
    for first in range(0, nodes, group):
        steps = range(first, first + group)
        shares.update(zip(steps, experts(*[blocks[s] for s in steps])))
    sums = []
    for step in range(0, nodes, 2):
        part = plus(shares[step], cross(shares[step + 1], 1))
        sums.append(cross(part, step) if step else part)
    return plus(*sums)


def solution(mesh):
    return jax.shard_map(
        per_device,
        mesh=mesh,
        in_specs=(
            P(("rep", "node", "local"), None),
            P(("rep", "node", "local"), None),
            P(("rep", "node", "local"), None),
            P("node", None, "local"),
            P("node", None, "local"),
            P("node", "local", None),
        ),
        out_specs=P(("rep", "node", "local"), None),
        check_vma=False,
    )
```
